256 devices in a mesh: section: 2 (over z_hi), dp: 32 (over x, z_lo, core), mp: 4 (over y).
Axes of the slice: x: 4, y: 4, z: 8 (z_hi: 2, z_lo: 4; z = z_hi * 4 + z_lo), core: 2. Of those that a mesh axis runs over, the one named last changes fastest.
Arguments:
- train_acts: bfloat16 [2, 4096, 4096], P('section', 'dp', 'mp'), may hold values from -6 to 6
- train_grads: bfloat16 [2, 4096, 14336], P('section', 'dp', 'mp'), may hold values from -6 to 6
- basis_in: bfloat16 [2, 4096, 512], P('section', 'mp'), may hold values from -0.25 to 0.25
- basis_out: bfloat16 [2, 14336, 512], P('section', 'mp'), may hold values from -0.25 to 0.25
- eigen_values: float32 [2, 4, 3584, 4096], P('section', None, 'dp', 'mp'), may hold values from 0.01 to 10
- query_acts: bfloat16 [2, 32, 32, 4096], P('section', 'dp', None, 'mp'), may hold values from -6 to 6
- query_grads: bfloat16 [2, 32, 32, 14336], P('section', 'dp', None, 'mp'), may hold values from -6 to 6
- query_owner: int32 [8], replicated, may hold values from 0 to 31, as said below
Outputs:
- influence: float32 [32, 8], P('dp')
The draws below stay inside these ranges and needn't reach their ends.
Inputs may be any that keep to these rules, and one draw needn't show every extreme that they name: `query_owner`: distinct slot numbers; slot s lies on index s // 1 of dp; slots that no query names hold unused data.
All inputs are finite; a program needn't handle non-finite values.
Results may differ from the reference program's by a relative error of at most 0.0056.
Values may be sent and summed in bfloat16 or wider, within the bound.
No kernel may reach another device: no remote copies, remote signals or barrier semaphores. Data moves between devices by JAX's collectives and lax.ppermute only.
A program may use at most 128 MiB of HBM per device.

```python
import math
import jax
import jax.numpy as jnp
from jax import lax

D = 4096
FF = 14336
BLOCK = 512
SEQLEN = 128
QUERIES = 8
QLEN = 32
LAYERS = 2
OWN_SLOTS = 1
OUT_GROUPS = 4
SEQUENCES = 32
TOKENS = 4096
N_DP = 32


def draw_query_owner(key, part):
    key = jax.random.fold_in(key, 7)
    slot_total = N_DP * OWN_SLOTS
    stride = slot_total // QUERIES
    ranking = jax.random.permutation(jax.random.fold_in(key, 1), QUERIES).astype(jnp.int32)
    offset = jax.random.randint(jax.random.fold_in(key, 2), (QUERIES,), 0, stride).astype(jnp.int32)
    offset = jnp.where(ranking == 0, 0, jnp.where(ranking == QUERIES - 1, stride - 1, offset))
    return (ranking * stride + offset).astype(jnp.int32)


def steps_of(key, dims, split, low, largest):
    gain = 1.0
    for dim, shards_of in split:
        heights = jax.random.uniform(jax.random.fold_in(jax.random.fold_in(key, 6), dim), (shards_of,), jnp.float32, low / len(split), largest / len(split))
        gain = gain * jnp.repeat(jnp.exp(heights), dims[dim] // shards_of).reshape((-1,) + (1,) * (len(dims) - 1 - dim))
    return gain


def bell_draw(own_key, extent, spread, limit, split=(), held_as=jnp.bfloat16):
    entries = jax.random.normal(own_key, extent, jnp.float32) * spread
    if len(split) > 0:
        entries = steps_of(own_key, extent, split, -0.22, 0.18) * entries
    return jnp.clip(entries, min=-limit, max=limit).astype(held_as)


def setup_inputs(seed: int = 0) -> dict:
    streams_of = jax.random.split(jax.random.key(seed), 9)
    train_acts = bell_draw(streams_of[0], (LAYERS, TOKENS, D), 1.0, 6.0, ((0, 2), (1, 32), (2, 4)))
    train_grads = bell_draw(streams_of[1], (LAYERS, TOKENS, FF), 1.0, 6.0, ((0, 2), (1, 32), (2, 4)))
    basis_in = bell_draw(streams_of[2], (LAYERS, D, BLOCK), BLOCK ** -0.5, 0.25, ((0, 2), (1, 4)))
    basis_out = bell_draw(streams_of[3], (LAYERS, FF, BLOCK), BLOCK ** -0.5, 0.25, ((0, 2), (1, 4)))
    eigen_values = jnp.clip(jnp.exp(math.log(10.0) - 6.9077553 * jax.random.uniform(streams_of[4], (LAYERS, OUT_GROUPS, FF // OUT_GROUPS, D), jnp.float32) ** steps_of(streams_of[4], (LAYERS, OUT_GROUPS, FF // OUT_GROUPS, D), ((0, 2), (2, 32), (3, 4)), -0.2, 0.2)), 0.01, 10.0)
    query_acts = bell_draw(streams_of[5], (LAYERS, N_DP * OWN_SLOTS, QLEN, D), 1.0, 6.0, ((0, 2), (1, 32), (3, 4)))
    query_grads = bell_draw(streams_of[6], (LAYERS, N_DP * OWN_SLOTS, QLEN, FF), 1.0, 6.0, ((0, 2), (1, 32), (3, 4)))
    query_owner = draw_query_owner(jax.random.fold_in(streams_of[8], 71), 0)
    return {"train_acts": train_acts, "train_grads": train_grads, "basis_in": basis_in, "basis_out": basis_out, "eigen_values": eigen_values, "query_acts": query_acts, "query_grads": query_grads, "query_owner": query_owner}


DAMPING = 0.1

def rotate(values, eigen_basis):
    row_count = values.shape[0]
    blocks = eigen_basis.shape[0] // BLOCK
    shaped = values.reshape(row_count, blocks, BLOCK).astype(jnp.float32)
    factor = eigen_basis.reshape(blocks, BLOCK, BLOCK).astype(jnp.float32)
    turned = jnp.einsum('rbk,bkc->rbc', shaped, factor)
    return turned.reshape(row_count, blocks * BLOCK).astype(jnp.bfloat16)

def rounded(values):
    return lax.optimization_barrier(values.astype(jnp.bfloat16)).astype(jnp.float32)

def layer_scores(acts, grads, basis_in, basis_out, values, query_acts, query_grads, query_owner):
    turned_acts = rotate(acts, basis_in).reshape(SEQUENCES, SEQLEN, D)
    grads_wide = rotate(grads, basis_out).astype(jnp.float32).reshape(SEQUENCES, SEQLEN, FF)
    slot_total = query_acts.shape[0]
    slot_acts = rotate(query_acts.reshape(slot_total * QLEN, D), basis_in).reshape(slot_total, QLEN, D)
    slot_grads = rotate(query_grads.reshape(slot_total * QLEN, FF), basis_out).reshape(slot_total, QLEN, FF)
    chosen_acts = jnp.take(slot_acts, query_owner, axis=0).astype(jnp.float32)
    chosen_grads = jnp.take(slot_grads, query_owner, axis=0).astype(jnp.float32)
    eigen_matrix = values.reshape(FF, D)
    column_span = min(128, D)

    def one_span(column_start):
        acts_span = lax.dynamic_slice_in_dim(turned_acts, column_start, column_span, 2).astype(jnp.float32)
        query_span = lax.dynamic_slice_in_dim(chosen_acts, column_start, column_span, 2)
        value_span = lax.dynamic_slice_in_dim(eigen_matrix, column_start, column_span, 1)
        moments = jnp.einsum('qsk,qsj->qkj', chosen_grads, query_span)
        weighted = rounded(moments / (value_span + DAMPING))
        gram_block = rounded(jnp.einsum('itk,itj->ikj', grads_wide, acts_span))
        return jnp.einsum('ikj,qkj->iq', gram_block, weighted)
    starts = (jnp.arange(D // column_span) * column_span).astype(jnp.int32)
    partial_sums = lax.map(one_span, starts)
    return lax.optimization_barrier(jnp.sum(partial_sums, axis=0))

def reference(train_acts, train_grads, basis_in, basis_out, eigen_values, query_acts, query_grads, query_owner):
    summed = jnp.zeros((SEQUENCES, QUERIES), jnp.float32)
    for layer_index in range(LAYERS):
        summed = summed + layer_scores(train_acts[layer_index], train_grads[layer_index], basis_in[layer_index], basis_out[layer_index], eigen_values[layer_index], query_acts[layer_index], query_grads[layer_index], query_owner)
    return summed / math.sqrt(LAYERS * D * FF * SEQLEN * QLEN)
```

```python
import functools
import math

import jax
import jax.numpy as jnp
from jax import lax
from jax.experimental import pallas as pl
from jax.experimental.pallas import tpu as pltpu
from jax.sharding import PartitionSpec as P

SEQLEN = 128
DAMPING = 0.1
ROWS = 16
CHUNK = 4
MIB = 1 << 20


def turn_acts_kernel(train_ref, query_ref, basis_ref, out_ref):
    size = basis_ref.shape[1]
    for b in range(train_ref.shape[1] // size):
        cols = slice(b * size, (b + 1) * size)
        rows = jnp.concatenate([train_ref[:, cols], query_ref[:, cols]], axis=0)
        out_ref[:, cols] = jnp.dot(
            rows, basis_ref[cols, :], preferred_element_type=jnp.float32
        ).astype(jnp.bfloat16)


def turn_grads_kernel(train_ref, query_ref, basis_ref, out_ref, turned, slots):
    step = pl.program_id(0)
    steps = pl.num_programs(0)
    size = basis_ref.shape[1]
    tokens = train_ref.shape[0]
    rows = jnp.concatenate([train_ref[...], query_ref[...]], axis=0)
    product = jnp.dot(rows, basis_ref[...], preferred_element_type=jnp.float32)
    turned[step] = product[:tokens].T.astype(jnp.bfloat16)
    slots[step] = product[tokens:]

    @pl.when(step == steps - 1)
    def _():
        pieces, _, lanes = out_ref.shape
        total = turned.shape[0] * size
        piece = total // pieces
        for d in range(pieces):
            start = d * piece
            parts = []
            at = start
            while at < start + piece:
                block = at // size
                end = min(start + piece, (block + 1) * size)
                parts.append(turned[block, at - block * size : end - block * size, :])
                at = end
            out_ref[d, :piece, :] = parts[0] if len(parts) == 1 else jnp.concatenate(parts, axis=0)
            first = start // lanes
            tiles = []
            for tile in range(first, min(first + 2, total // lanes)):
                col = tile * lanes
                block = col // size
                tiles.append(slots[block, :, col - block * size : col - block * size + lanes])
            window = jnp.concatenate(tiles, axis=1) if len(tiles) > 1 else tiles[0]
            shift = start - first * lanes
            if shift:
                window = pltpu.roll(window, window.shape[1] - shift, 1)
            out_ref[d, piece:, :] = window[:, :lanes].astype(jnp.bfloat16)


def weigh_kernel(order_ref, owner_ref, grads_ref, *refs):
    queries = owner_ref.shape[0]
    slot_refs = refs[:queries]
    lambda_ref, out_ref, acts = refs[queries:]
    length = slot_refs[0].shape[1]

    @pl.when(pl.program_id(0) == 0)
    def _():
        for q in range(queries):
            acts[q * length : (q + 1) * length, :] = slot_refs[q][0]

    turned = grads_ref[0].astype(jnp.float32).T.astype(jnp.bfloat16)
    shape = (queries * ROWS, queries * length)
    own = (
        lax.broadcasted_iota(jnp.int32, shape, 0) // ROWS
        == lax.broadcasted_iota(jnp.int32, shape, 1) // length
    )
    for b in range(lambda_ref.shape[1] // ROWS):
        rows = slice(b * ROWS, (b + 1) * ROWS)
        spread = jnp.concatenate([turned[rows].astype(jnp.float32)] * queries, axis=0)
        spread = jnp.where(own, spread, 0.0).astype(jnp.bfloat16)
        moments = jnp.dot(spread, acts[...], preferred_element_type=jnp.float32)
        inverse = 1.0 / (lambda_ref[0, rows, :] + DAMPING)
        moments = moments.reshape(queries, ROWS, moments.shape[1]) * inverse[None]
        out_ref[0, b] = moments.reshape(queries * ROWS, moments.shape[2]).astype(jnp.bfloat16)


def score_kernel(grads_ref, acts_ref, weighted_ref, out_ref, grams):
    step = pl.program_id(0)
    steps = pl.num_programs(0)
    blocks = weighted_ref.shape[1]
    for i in range(CHUNK):
        gram = jnp.dot(grads_ref[i], acts_ref[i], preferred_element_type=jnp.float32)
        gram = gram.astype(jnp.bfloat16)
        start = pl.multiple_of((step * CHUNK + i) * ROWS, ROWS)
        for b in range(blocks):
            grams[b, pl.ds(start, ROWS), :] = gram[b * ROWS : (b + 1) * ROWS]

    @pl.when(step == steps - 1)
    def _():
        total = jnp.zeros((grams.shape[1], weighted_ref.shape[2]), jnp.float32)
        for b in range(blocks):
            total += lax.dot_general(
                grams[b],
                weighted_ref[0, b],
                (((1,), (1,)), ((), ())),
                preferred_element_type=jnp.float32,
            )
        same = (
            lax.broadcasted_iota(jnp.int32, total.shape, 0) % ROWS
            == lax.broadcasted_iota(jnp.int32, total.shape, 1) % ROWS
        )
        total = jnp.where(same, total, 0.0)
        out_ref[...] = jnp.sum(total.reshape(-1, ROWS, total.shape[1]), axis=1)


def per_device(
    train_acts, train_grads, basis_in, basis_out, eigen_values, query_acts, query_grads, query_owner
):
    block_size = basis_in.shape[2]
    tokens, act_cols = train_acts.shape[1:]
    grad_cols = train_grads.shape[2]
    length = query_acts.shape[2]
    queries = query_owner.shape[0]
    data_size = lax.axis_size("dp")
    model_size = lax.axis_size("mp")
    piece = grad_cols // data_size
    sequences = data_size * tokens // SEQLEN
    bf16 = jnp.bfloat16

    turned_acts = pl.pallas_call(
        turn_acts_kernel,
        out_shape=jax.ShapeDtypeStruct((tokens + length, act_cols), bf16),
        compiler_params=pltpu.CompilerParams(vmem_limit_bytes=24 * MIB),
        name="turn_acts",
    )(train_acts[0], query_acts[0, 0], basis_in[0])
    all_acts = lax.all_gather(turned_acts, "dp", axis=0)

    steps = grad_cols // block_size
    pieces = pl.pallas_call(
        turn_grads_kernel,
        grid=(steps,),
        in_specs=[
            pl.BlockSpec((tokens, block_size), lambda s: (0, s)),
            pl.BlockSpec((length, block_size), lambda s: (0, s)),
            pl.BlockSpec((block_size, block_size), lambda s: (s, 0)),
        ],
        out_specs=pl.BlockSpec((data_size, piece + length, tokens), lambda s: (0, 0, 0)),
        out_shape=jax.ShapeDtypeStruct((data_size, piece + length, tokens), bf16),
        scratch_shapes=[
            pltpu.VMEM((steps, block_size, tokens), bf16),
            pltpu.VMEM((steps, length, block_size), jnp.float32),
        ],
        compiler_params=pltpu.CompilerParams(vmem_limit_bytes=24 * MIB),
        name="turn_grads",
    )(train_grads[0], query_grads[0, 0], basis_out[0])
    moved = lax.all_to_all(pieces, "dp", split_axis=0, concat_axis=0, tiled=True)
    own_grads = moved[:, :piece]
    own_query = jnp.take(moved[:, piece:], query_owner, axis=0).reshape(queries * length, tokens)

    ring = range(model_size)
    shifts = [[(i, (i + s) % model_size) for i in ring] for s in (1, model_size - 1, 2)]
    query_parts = [own_query] + [lax.ppermute(own_query, "mp", pairs) for pairs in shifts]
    grad_parts = [own_grads] + [lax.ppermute(own_grads, "mp", pairs) for pairs in shifts]
    model_index = lax.axis_index("mp")
    order = jnp.stack([(model_index + s) % model_size for s in (0, model_size - 1, 1, 2)])
    order = order.astype(jnp.int32)

    blocks = piece // ROWS
    slot_specs = [
        pl.BlockSpec((1, length, act_cols), functools.partial(
            lambda q, s, order, owner: (owner[q], tokens // length, 0), q))
        for q in range(queries)
    ]
    weighted = pl.pallas_call(
        weigh_kernel,
        grid_spec=pltpu.PrefetchScalarGridSpec(
            num_scalar_prefetch=2,
            grid=(model_size,),
            in_specs=[
                pl.BlockSpec((1, queries * length, tokens), lambda s, order, owner: (s, 0, 0)),
                *slot_specs,
                pl.BlockSpec((1, piece, act_cols), lambda s, order, owner: (order[s], 0, 0)),
            ],
            out_specs=pl.BlockSpec(
                (1, blocks, queries * ROWS, act_cols), lambda s, order, owner: (s, 0, 0, 0)
            ),
            scratch_shapes=[pltpu.VMEM((queries * length, act_cols), bf16)],
        ),
        out_shape=jax.ShapeDtypeStruct((model_size, blocks, queries * ROWS, act_cols), bf16),
        compiler_params=pltpu.CompilerParams(vmem_limit_bytes=32 * MIB),
        name="weigh",
    )(order, query_owner, jnp.stack(query_parts), *([all_acts] * queries), eigen_values[0])

    def score(part, grads):
        return pl.pallas_call(
            score_kernel,
            grid=(sequences // CHUNK,),
            in_specs=[
                pl.BlockSpec((CHUNK, piece, tokens), lambda s: (s, 0, 0)),
                pl.BlockSpec((CHUNK, tokens, act_cols), lambda s: (s, 0, 0)),
                pl.BlockSpec(
                    (1, blocks, queries * ROWS, act_cols), lambda s: (part, 0, 0, 0)
                ),
            ],
            out_specs=pl.BlockSpec((sequences, queries * ROWS), lambda s: (0, 0)),
            out_shape=jax.ShapeDtypeStruct((sequences, queries * ROWS), jnp.float32),
            scratch_shapes=[pltpu.VMEM((blocks, sequences * ROWS, act_cols), bf16)],
            compiler_params=pltpu.CompilerParams(vmem_limit_bytes=40 * MIB),
            name="score",
        )(grads, all_acts, weighted)

    scores = sum(score(part, grads) for part, grads in enumerate(grad_parts))
    partial = scores.reshape(sequences, queries, ROWS).sum(axis=2)

    mine = lax.all_to_all(partial, "dp", split_axis=0, concat_axis=0, tiled=True).sum(axis=0)
    others = model_size * lax.axis_size("section")
    spread = jnp.broadcast_to(mine[None], (others, queries))
    gathered = lax.all_to_all(spread, ("section", "mp"), split_axis=0, concat_axis=0, tiled=True)
    layers = train_acts.shape[0] * lax.axis_size("section")
    normalizer = math.sqrt(
        layers * act_cols * model_size * grad_cols * model_size * SEQLEN * length
    )
    return gathered.sum(axis=0, keepdims=True) / normalizer


def solution(mesh):
    in_specs = (
        P("section", "dp", "mp"),
        P("section", "dp", "mp"),
        P("section", "mp", None),
        P("section", "mp", None),
        P("section", None, "dp", "mp"),
        P("section", "dp", None, "mp"),
        P("section", "dp", None, "mp"),
        P(),
    )
    return jax.shard_map(
        per_device, mesh=mesh, in_specs=in_specs, out_specs=P("dp", None), check_vma=False
    )
```

```python
import functools
import math

import jax
import jax.numpy as jnp
from jax import lax
from jax.experimental import pallas as pl
from jax.experimental.pallas import tpu as pltpu
from jax.sharding import PartitionSpec as P

SEQLEN = 128
DAMPING = 0.1
ROWS = 16
CHUNK = 4
MIB = 1 << 20


def turn_acts_kernel(train_ref, query_ref, basis_ref, out_ref):
    rows = jnp.concatenate([train_ref[...], query_ref[...]], axis=0)
    out_ref[...] = jnp.dot(
        rows, basis_ref[...], preferred_element_type=jnp.float32
    ).astype(jnp.bfloat16)


def turn_grads_kernel(train_ref, query_ref, basis_ref, out_ref, turned, slots):
    step = pl.program_id(0)
    steps = pl.num_programs(0)
    size = basis_ref.shape[1]
    tokens = train_ref.shape[0]
    rows = jnp.concatenate([train_ref[...], query_ref[...]], axis=0)
    product = jnp.dot(rows, basis_ref[...], preferred_element_type=jnp.float32)
    turned[step] = product[:tokens].T.astype(jnp.bfloat16)
    slots[step] = product[tokens:]

    @pl.when(step == steps - 1)
    def _():
        pieces, _, lanes = out_ref.shape
        total = turned.shape[0] * size
        piece = total // pieces
        for d in range(pieces):
            start = d * piece
            parts = []
            at = start
            while at < start + piece:
                block = at // size
                end = min(start + piece, (block + 1) * size)
                parts.append(turned[block, at - block * size : end - block * size, :])
                at = end
            out_ref[d, :piece, :] = parts[0] if len(parts) == 1 else jnp.concatenate(parts, axis=0)
            first = start // lanes
            tiles = []
            for tile in range(first, min(first + 2, total // lanes)):
                col = tile * lanes
                block = col // size
                tiles.append(slots[block, :, col - block * size : col - block * size + lanes])
            window = jnp.concatenate(tiles, axis=1) if len(tiles) > 1 else tiles[0]
            shift = start - first * lanes
            if shift:
                window = pltpu.roll(window, window.shape[1] - shift, 1)
            out_ref[d, piece:, :] = window[:, :lanes].astype(jnp.bfloat16)


def weigh_kernel(order_ref, owner_ref, grads_ref, *refs):
    queries = owner_ref.shape[0]
    slot_refs = refs[:queries]
    lambda_ref, out_ref, acts = refs[queries:]
    length = slot_refs[0].shape[1]

    @pl.when(pl.program_id(0) == 0)
    def _():
        for q in range(queries):
            acts[q * length : (q + 1) * length, :] = slot_refs[q][0]

    turned = grads_ref[0].astype(jnp.float32).T.astype(jnp.bfloat16)
    shape = (queries * ROWS, queries * length)
    own = (
        lax.broadcasted_iota(jnp.int32, shape, 0) // ROWS
        == lax.broadcasted_iota(jnp.int32, shape, 1) // length
    )
    for b in range(lambda_ref.shape[1] // ROWS):
        rows = slice(b * ROWS, (b + 1) * ROWS)
        spread = jnp.concatenate([turned[rows].astype(jnp.float32)] * queries, axis=0)
        spread = jnp.where(own, spread, 0.0).astype(jnp.bfloat16)
        moments = jnp.dot(spread, acts[...], preferred_element_type=jnp.float32)
        inverse = 1.0 / (lambda_ref[0, rows, :] + DAMPING)
        moments = moments.reshape(queries, ROWS, moments.shape[1]) * inverse[None]
        out_ref[0, b] = moments.reshape(queries * ROWS, moments.shape[2]).astype(jnp.bfloat16)


def score_kernel(*refs):
    parts = len(refs) - 7
    part_refs = refs[:parts]
    acts_ref, weighted_ref, out_ref, grams, weighted, totals, arrived = refs[parts:]
    step = pl.program_id(0)
    steps = pl.num_programs(0)
    blocks = weighted.shape[0]
    load = pltpu.make_async_copy(weighted_ref, weighted, arrived)

    @pl.when(step == 0)
    def _():
        load.start()

    for i in range(CHUNK):
        grads = jnp.concatenate([part[i] for part in part_refs], axis=0)
        gram = jnp.dot(grads, acts_ref[i], preferred_element_type=jnp.float32)
        gram = gram.astype(jnp.bfloat16)
        start = pl.multiple_of((step * CHUNK + i) * ROWS, ROWS)
        for b in range(blocks):
            grams[b, pl.ds(start, ROWS), :] = gram[b * ROWS : (b + 1) * ROWS]

    @pl.when(step == steps - 1)
    def _():
        load.wait()
        totals[...] = jnp.zeros_like(totals)
        group = 7

        @pl.loop(0, blocks // group)
        def _(g):
            for b in range(group):
                totals[...] += lax.dot_general(
                    grams[g * group + b],
                    weighted[g * group + b],
                    (((1,), (1,)), ((), ())),
                    preferred_element_type=jnp.float32,
                )

        shape = totals.shape
        same = (
            lax.broadcasted_iota(jnp.int32, shape, 0) % ROWS
            == lax.broadcasted_iota(jnp.int32, shape, 1) % ROWS
        )
        kept = jnp.where(same, totals[...], 0.0)
        out_ref[...] = jnp.sum(kept.reshape(-1, ROWS, shape[1]), axis=1)


def per_device(
    train_acts, train_grads, basis_in, basis_out, eigen_values, query_acts, query_grads, query_owner
):
    block_size = basis_in.shape[2]
    tokens, act_cols = train_acts.shape[1:]
    grad_cols = train_grads.shape[2]
    length = query_acts.shape[2]
    queries = query_owner.shape[0]
    data_size = lax.axis_size("dp")
    model_size = lax.axis_size("mp")
    piece = grad_cols // data_size
    sequences = data_size * tokens // SEQLEN
    bf16 = jnp.bfloat16

    turned_acts = pl.pallas_call(
        turn_acts_kernel,
        grid=(act_cols // block_size,),
        in_specs=[
            pl.BlockSpec((tokens, block_size), lambda s: (0, s)),
            pl.BlockSpec((length, block_size), lambda s: (0, s)),
            pl.BlockSpec((block_size, block_size), lambda s: (s, 0)),
        ],
        out_specs=pl.BlockSpec((tokens + length, block_size), lambda s: (0, s)),
        out_shape=jax.ShapeDtypeStruct((tokens + length, act_cols), bf16),
        compiler_params=pltpu.CompilerParams(vmem_limit_bytes=60 * MIB),
        name="turn_acts",
    )(train_acts[0], query_acts[0, 0], basis_in[0])
    all_acts = lax.all_gather(turned_acts, "dp", axis=0)

    steps = grad_cols // block_size
    pieces = pl.pallas_call(
        turn_grads_kernel,
        grid=(steps,),
        in_specs=[
            pl.BlockSpec((tokens, block_size), lambda s: (0, s)),
            pl.BlockSpec((length, block_size), lambda s: (0, s)),
            pl.BlockSpec((block_size, block_size), lambda s: (s, 0)),
        ],
        out_specs=pl.BlockSpec((data_size, piece + length, tokens), lambda s: (0, 0, 0)),
        out_shape=jax.ShapeDtypeStruct((data_size, piece + length, tokens), bf16),
        scratch_shapes=[
            pltpu.VMEM((steps, block_size, tokens), bf16),
            pltpu.VMEM((steps, length, block_size), jnp.float32),
        ],
        compiler_params=pltpu.CompilerParams(vmem_limit_bytes=60 * MIB),
        name="turn_grads",
    )(train_grads[0], query_grads[0, 0], basis_out[0])
    moved = lax.all_to_all(pieces, "dp", split_axis=0, concat_axis=0, tiled=True)
    own_grads = moved[:, :piece]
    own_query = jnp.take(moved[:, piece:], query_owner, axis=0).reshape(queries * length, tokens)

    ring = range(model_size)
    shifts = [[(i, (i + s) % model_size) for i in ring] for s in (1, model_size - 1, 2)]
    query_parts = [own_query] + [lax.ppermute(own_query, "mp", pairs) for pairs in shifts]
    grad_parts = [own_grads] + [lax.ppermute(own_grads, "mp", pairs) for pairs in shifts]
    model_index = lax.axis_index("mp")
    order = jnp.stack([(model_index + s) % model_size for s in (0, model_size - 1, 1, 2)])
    order = order.astype(jnp.int32)

    blocks = piece // ROWS
    slot_specs = [
        pl.BlockSpec((1, length, act_cols), functools.partial(
            lambda q, s, order, owner: (owner[q], tokens // length, 0), q))
        for q in range(queries)
    ]
    weighted = pl.pallas_call(
        weigh_kernel,
        grid_spec=pltpu.PrefetchScalarGridSpec(
            num_scalar_prefetch=2,
            grid=(model_size,),
            in_specs=[
                pl.BlockSpec((1, queries * length, tokens), lambda s, order, owner: (s, 0, 0)),
                *slot_specs,
                pl.BlockSpec((1, piece, act_cols), lambda s, order, owner: (order[s], 0, 0)),
            ],
            out_specs=pl.BlockSpec(
                (1, blocks, queries * ROWS, act_cols), lambda s, order, owner: (s, 0, 0, 0)
            ),
            scratch_shapes=[pltpu.VMEM((queries * length, act_cols), bf16)],
        ),
        out_shape=jax.ShapeDtypeStruct((model_size, blocks, queries * ROWS, act_cols), bf16),
        compiler_params=pltpu.CompilerParams(vmem_limit_bytes=60 * MIB),
        name="weigh",
    )(order, query_owner, jnp.stack(query_parts), *([all_acts] * queries), eigen_values[0])

    weighted = weighted.reshape(model_size * blocks, queries * ROWS, act_cols)
    part_spec = pl.BlockSpec((CHUNK, piece, tokens), lambda s: (s, 0, 0))
    scores = pl.pallas_call(
        score_kernel,
        grid=(sequences // CHUNK,),
        in_specs=[part_spec] * model_size
        + [
            pl.BlockSpec((CHUNK, tokens, act_cols), lambda s: (s, 0, 0)),
            pl.BlockSpec(memory_space=pl.ANY),
        ],
        out_specs=pl.BlockSpec((sequences, queries * ROWS), lambda s: (0, 0)),
        out_shape=jax.ShapeDtypeStruct((sequences, queries * ROWS), jnp.float32),
        scratch_shapes=[
            pltpu.VMEM((model_size * blocks, sequences * ROWS, act_cols), bf16),
            pltpu.VMEM(weighted.shape, bf16),
            pltpu.VMEM((sequences * ROWS, queries * ROWS), jnp.float32),
            pltpu.SemaphoreType.DMA,
        ],
        compiler_params=pltpu.CompilerParams(vmem_limit_bytes=60 * MIB),
        name="score",
    )(*grad_parts, all_acts, weighted)
    partial = scores.reshape(sequences, queries, ROWS).sum(axis=2)

    mine = lax.all_to_all(partial, "dp", split_axis=0, concat_axis=0, tiled=True).sum(axis=0)
    others = model_size * lax.axis_size("section")
    spread = jnp.broadcast_to(mine[None], (others, queries))
    gathered = lax.all_to_all(spread, ("section", "mp"), split_axis=0, concat_axis=0, tiled=True)
    layers = train_acts.shape[0] * lax.axis_size("section")
    normalizer = math.sqrt(
        layers * act_cols * model_size * grad_cols * model_size * SEQLEN * length
    )
    return gathered.sum(axis=0, keepdims=True) / normalizer


def solution(mesh):
    in_specs = (
        P("section", "dp", "mp"),
        P("section", "dp", "mp"),
        P("section", "mp", None),
        P("section", "mp", None),
        P("section", None, "dp", "mp"),
        P("section", "dp", None, "mp"),
        P("section", "dp", None, "mp"),
        P(),
    )
    return jax.shard_map(
        per_device, mesh=mesh, in_specs=in_specs, out_specs=P("dp", None), check_vma=False
    )
```

```python
import functools
import math

import jax
import jax.numpy as jnp
from jax import lax
from jax.experimental import pallas as pl
from jax.experimental.pallas import tpu as pltpu
from jax.sharding import PartitionSpec as P

SEQLEN = 128
DAMPING = 0.1
ROWS = 16
CORES = 2
DEPTH = 4
MIB = 1 << 20


def tile_of(target, side):
    x, rest = divmod(target, DEPTH)
    z, core = divmod(rest, CORES)
    return (x * DEPTH + 2 * z + side) * CORES + core


def turn_acts_kernel(train_ref, query_ref, basis_ref, out_ref):
    rows = jnp.concatenate([train_ref[...], query_ref[...]], axis=0)
    out_ref[...] = jnp.dot(
        rows, basis_ref[...], preferred_element_type=jnp.float32
    ).astype(jnp.bfloat16)


def turn_grads_kernel(train_ref, query_ref, basis_ref, out_ref, turned, slots):
    step = pl.program_id(0)
    steps = pl.num_programs(0)
    size = basis_ref.shape[1]
    tokens = train_ref.shape[0]
    rows = jnp.concatenate([train_ref[...], query_ref[...]], axis=0)
    product = jnp.dot(rows, basis_ref[...], preferred_element_type=jnp.float32)
    turned[step] = product[:tokens].T.astype(jnp.bfloat16)
    slots[step] = product[tokens:]

    @pl.when(step == steps - 1)
    def _():
        targets, _, lanes = out_ref.shape
        total = turned.shape[0] * size
        piece = total // (2 * targets)
        length = slots.shape[1]
        for target in range(targets):
            for side in range(2):
                start = tile_of(target, side) * piece
                parts = []
                at = start
                while at < start + piece:
                    block = at // size
                    end = min(start + piece, (block + 1) * size)
                    parts.append(turned[block, at - block * size : end - block * size, :])
                    at = end
                rows = parts[0] if len(parts) == 1 else jnp.concatenate(parts, axis=0)
                out_ref[target, side * piece : (side + 1) * piece, :] = rows
                first = start // lanes
                tiles = []
                for tile in range(first, min(first + 2, total // lanes)):
                    col = tile * lanes
                    block = col // size
                    tiles.append(slots[block, :, col - block * size : col - block * size + lanes])
                window = jnp.concatenate(tiles, axis=1) if len(tiles) > 1 else tiles[0]
                shift = start - first * lanes
                if shift:
                    window = pltpu.roll(window, window.shape[1] - shift, 1)
                at = 2 * piece + side * length
                out_ref[target, at : at + length, :] = window[:, :lanes].astype(jnp.bfloat16)


def weigh_kernel(order_ref, place_ref, grads_ref, *refs):
    acts_refs = refs[:-4]
    own_ref, other_ref, out_ref, acts = refs[-4:]
    count = acts_refs[0].shape[2]
    tokens = len(acts_refs) * count
    queries = out_ref.shape[2] // ROWS

    @pl.when(pl.program_id(0) == 0)
    def _():
        for n, ref in enumerate(acts_refs):
            at = pl.multiple_of(place_ref[n] * count, count)
            acts[pl.ds(at, count), :] = ref[0, 0]

    turned = grads_ref[0].astype(jnp.float32).T
    shape = (queries * ROWS, tokens)
    own = lax.broadcasted_iota(jnp.int32, shape, 0) // ROWS == (
        lax.broadcasted_iota(jnp.int32, shape, 1) // (count // queries)
    ) % queries
    blocks = own_ref.shape[1] // ROWS
    lanes = grads_ref.shape[2] // 2
    side_of_own = place_ref[len(acts_refs)]
    for side in range(2):
        mine = side_of_own == side
        for b in range(blocks):
            rows = slice(b * ROWS, (b + 1) * ROWS)
            part = turned[side * lanes + b * ROWS : side * lanes + (b + 1) * ROWS]
            spread = jnp.concatenate([part] * queries, axis=0)
            spread = jnp.where(own, spread, 0.0).astype(jnp.bfloat16)
            moments = jnp.dot(spread, acts[...], preferred_element_type=jnp.float32)
            values = jnp.where(mine, own_ref[0, rows, :], other_ref[0, rows, :].astype(jnp.float32))
            inverse = 1.0 / (values + DAMPING)
            moments = moments.reshape(queries, ROWS, moments.shape[1]) * inverse[None]
            moments = moments.reshape(queries * ROWS, moments.shape[2])
            out_ref[0, side * blocks + b] = moments.astype(jnp.bfloat16)


def score_kernel(first, place_ref, *refs):
    parts = len(refs) - 8
    part_refs = refs[:parts]
    near_ref, far_ref, weighted_ref, out_ref, grams, weighted, totals, arrived = refs[parts:]
    step = pl.program_id(0)
    steps = pl.num_programs(0)
    blocks = weighted.shape[0]
    load = pltpu.make_async_copy(weighted_ref.at[pl.ds(first, blocks)], weighted, arrived)

    @pl.when(step == 0)
    def _():
        load.start()

    pairs = near_ref.shape[1]
    for far, acts_ref in enumerate((near_ref, far_ref)):
        for n in range(pairs):
            place = place_ref[(far * steps + step) * pairs + n]
            inner = lax.rem(place, CORES * pairs)
            grads = jnp.concatenate([part[0, inner] for part in part_refs], axis=0)
            gram = jnp.dot(grads, acts_ref[0, n], preferred_element_type=jnp.float32)
            gram = gram.astype(jnp.bfloat16)
            start = pl.multiple_of(place * ROWS, ROWS)
            for b in range(blocks):
                grams[b, pl.ds(start, ROWS), :] = gram[b * ROWS : (b + 1) * ROWS]

    @pl.when(step == steps - 1)
    def _():
        load.wait()
        totals[...] = jnp.zeros_like(totals)
        group = 7

        @pl.loop(0, blocks // group)
        def _(g):
            for b in range(group):
                totals[...] += lax.dot_general(
                    grams[g * group + b],
                    weighted[g * group + b],
                    (((1,), (1,)), ((), ())),
                    preferred_element_type=jnp.float32,
                )

        shape = totals.shape
        same = (
            lax.broadcasted_iota(jnp.int32, shape, 0) % ROWS
            == lax.broadcasted_iota(jnp.int32, shape, 1) % ROWS
        )
        kept = jnp.where(same, totals[...], 0.0)
        out_ref[...] = jnp.sum(kept.reshape(-1, ROWS, shape[1]), axis=1)


def per_device(
    train_acts, train_grads, basis_in, basis_out, eigen_values, query_acts, query_grads, query_owner
):
    block_size = basis_in.shape[2]
    tokens, act_cols = train_acts.shape[1:]
    grad_cols = train_grads.shape[2]
    length = query_acts.shape[2]
    queries = query_owner.shape[0]
    data_size = lax.axis_size("dp")
    model_size = lax.axis_size("mp")
    piece = grad_cols // data_size
    bf16 = jnp.bfloat16

    turned_acts = pl.pallas_call(
        turn_acts_kernel,
        grid=(act_cols // block_size,),
        in_specs=[
            pl.BlockSpec((tokens, block_size), lambda s: (0, s)),
            pl.BlockSpec((length, block_size), lambda s: (0, s)),
            pl.BlockSpec((block_size, block_size), lambda s: (s, 0)),
        ],
        out_specs=pl.BlockSpec((tokens + length, block_size), lambda s: (0, s)),
        out_shape=jax.ShapeDtypeStruct((tokens + length, act_cols), bf16),
        compiler_params=pltpu.CompilerParams(vmem_limit_bytes=60 * MIB),
        name="turn_acts",
    )(train_acts[0], query_acts[0, 0], basis_in[0])
    width = data_size // (DEPTH * CORES)
    targets = data_size // 2
    classes = [[tile_of(t, parity) for t in range(targets)] for parity in range(2)]
    where = [(x, z, c) for x in range(width) for z in range(DEPTH) for c in range(CORES)]

    def shifted(dx=0, dz=0, flip_z=0, flip_c=0):
        at = lambda x, z, c: (x % width * DEPTH + z % DEPTH) * CORES + c
        return [
            (at(x, z, c), at(x + dx, (z + dz) % DEPTH ^ flip_z, c ^ flip_c)) for x, z, c in where
        ]

    data_index = lax.axis_index("dp")
    my_x = data_index // (DEPTH * CORES)
    my_z = data_index // CORES % DEPTH
    my_core = data_index % CORES
    my_class = my_z % 2

    other_values = lax.ppermute(eigen_values[0].astype(bf16), "dp", shifted(flip_z=1))

    each = length // targets
    slot_acts = turned_acts[tokens:].reshape(width, DEPTH // 2, 1, CORES, -1, tokens)
    slot_acts = jnp.broadcast_to(slot_acts, (width, DEPTH // 2, 2, CORES) + slot_acts.shape[4:])
    slot_acts = slot_acts.reshape(data_size, -1, tokens)
    slot_acts = lax.all_to_all(slot_acts, "dp", split_axis=0, concat_axis=0, tiled=True)
    chosen_acts = jnp.take(slot_acts, query_owner, axis=0).reshape(queries * each, act_cols)
    sent = jnp.concatenate([turned_acts[:tokens], chosen_acts], axis=0)
    pair = jnp.stack([sent, lax.ppermute(sent, "dp", shifted(dz=2))])

    steps = grad_cols // block_size
    rows = 2 * (piece + length)
    pieces = pl.pallas_call(
        turn_grads_kernel,
        grid=(steps,),
        in_specs=[
            pl.BlockSpec((tokens, block_size), lambda s: (0, s)),
            pl.BlockSpec((length, block_size), lambda s: (0, s)),
            pl.BlockSpec((block_size, block_size), lambda s: (s, 0)),
        ],
        out_specs=pl.BlockSpec((targets, rows, tokens), lambda s: (0, 0, 0)),
        out_shape=jax.ShapeDtypeStruct((targets, rows, tokens), bf16),
        scratch_shapes=[
            pltpu.VMEM((steps, block_size, tokens), bf16),
            pltpu.VMEM((steps, length, block_size), jnp.float32),
        ],
        compiler_params=pltpu.CompilerParams(vmem_limit_bytes=60 * MIB),
        name="turn_grads",
    )(train_grads[0], query_grads[0, 0], basis_out[0])
    moved = lax.all_to_all(
        pieces, "dp", split_axis=0, concat_axis=0, tiled=True, axis_index_groups=classes
    )
    own_grads = moved[:, : 2 * piece].reshape(width, DEPTH // 2 * CORES, 2 * piece, tokens)

    owner_z = query_owner // CORES % DEPTH
    owner_place = query_owner // (DEPTH * CORES) * DEPTH + owner_z // 2 * CORES
    owner_place = owner_place + query_owner % CORES
    chosen = jnp.take(moved[:, 2 * piece :], owner_place, axis=0)
    chosen = jnp.where((owner_z % 2 == my_class)[:, None, None], chosen, 0).astype(bf16)
    chosen = chosen.reshape(queries, 2, targets, each, tokens).transpose(2, 0, 3, 1, 4)
    chosen = chosen.reshape(queries * length, 2 * tokens)
    own_query = chosen + lax.ppermute(chosen, "dp", shifted(flip_z=1))

    ring = range(model_size)
    shifts = [[(i, (i + s) % model_size) for i in ring] for s in (1, model_size - 1, 2)]
    grad_parts = [own_grads] + [lax.ppermute(own_grads, "mp", pairs) for pairs in shifts]
    query_parts = [own_query] + [lax.ppermute(own_query, "mp", pairs) for pairs in shifts]
    model_index = lax.axis_index("mp")
    order = jnp.stack([(model_index + s) % model_size for s in (0, model_size - 1, 1, 2)])
    order = order.astype(jnp.int32)

    near = jnp.stack([pair] + [lax.ppermute(pair, "dp", shifted(dx=s)) for s in range(1, width)])
    far = lax.ppermute(near, "dp", shifted(flip_c=1))
    places = [
        ((my_x + width - s) % width * (DEPTH // 2) + (my_z // 2 + n) % 2) * CORES
        + (my_core + flip) % CORES
        for flip in range(2)
        for s in range(width)
        for n in range(2)
    ]
    place = jnp.stack(places + [my_class]).astype(jnp.int32)

    blocks = piece // ROWS
    acts_specs = [
        pl.BlockSpec((1, 1, queries * each, act_cols), functools.partial(
            lambda x, n, s, order, place: (x, n, tokens // (queries * each), 0), x, n))
        for x in range(width)
        for n in range(2)
    ]
    weighted = pl.pallas_call(
        weigh_kernel,
        grid_spec=pltpu.PrefetchScalarGridSpec(
            num_scalar_prefetch=2,
            grid=(model_size,),
            in_specs=[
                pl.BlockSpec((1, queries * length, 2 * tokens), lambda s, order, place: (s, 0, 0)),
                *acts_specs,
                *acts_specs,
                pl.BlockSpec((1, piece, act_cols), lambda s, order, place: (order[s], 0, 0)),
                pl.BlockSpec((1, piece, act_cols), lambda s, order, place: (order[s], 0, 0)),
            ],
            out_specs=pl.BlockSpec(
                (1, 2 * blocks, queries * ROWS, act_cols), lambda s, order, place: (s, 0, 0, 0)
            ),
            scratch_shapes=[pltpu.VMEM((queries * length, act_cols), bf16)],
        ),
        out_shape=jax.ShapeDtypeStruct((model_size, 2 * blocks, queries * ROWS, act_cols), bf16),
        compiler_params=pltpu.CompilerParams(vmem_limit_bytes=60 * MIB),
        name="weigh",
    )(
        order, place, jnp.stack(query_parts), *([near] * (2 * width)), *([far] * (2 * width)),
        eigen_values[0], other_values,
    )
    weighted = weighted.reshape(model_size * 2 * blocks, queries * ROWS, act_cols)

    def score(first, parts):
        count = len(parts) * 2 * blocks
        part_spec = pl.BlockSpec(
            (1,) + own_grads.shape[1:],
            lambda s, place: (lax.div(place[2 * s], DEPTH // 2 * CORES), 0, 0, 0),
        )
        acts_spec = pl.BlockSpec((1, 2, tokens, act_cols), lambda s, place: (s, 0, 0, 0))
        return pl.pallas_call(
            functools.partial(score_kernel, first * 2 * blocks),
            grid_spec=pltpu.PrefetchScalarGridSpec(
                num_scalar_prefetch=1,
                grid=(width,),
                in_specs=[part_spec] * len(parts)
                + [acts_spec, acts_spec, pl.BlockSpec(memory_space=pl.ANY)],
                out_specs=pl.BlockSpec((targets, queries * ROWS), lambda s, place: (0, 0)),
                scratch_shapes=[
                    pltpu.VMEM((count, targets * ROWS, act_cols), bf16),
                    pltpu.VMEM((count,) + weighted.shape[1:], bf16),
                    pltpu.VMEM((targets * ROWS, queries * ROWS), jnp.float32),
                    pltpu.SemaphoreType.DMA,
                ],
            ),
            out_shape=jax.ShapeDtypeStruct((targets, queries * ROWS), jnp.float32),
            compiler_params=pltpu.CompilerParams(vmem_limit_bytes=60 * MIB),
            name="score",
        )(place, *parts, near, far, weighted)

    scores = score(0, grad_parts[:3]) + score(3, grad_parts[3:])
    partial = scores.reshape(targets, queries, ROWS).sum(axis=2)

    mine = lax.all_to_all(
        partial, "dp", split_axis=0, concat_axis=0, tiled=True, axis_index_groups=classes
    ).sum(axis=0)
    others = model_size * lax.axis_size("section")
    spread = jnp.broadcast_to(mine[None], (others, queries))
    gathered = lax.all_to_all(spread, ("section", "mp"), split_axis=0, concat_axis=0, tiled=True)
    layers = train_acts.shape[0] * lax.axis_size("section")
    normalizer = math.sqrt(
        layers * act_cols * model_size * grad_cols * model_size * SEQLEN * length
    )
    return gathered.sum(axis=0, keepdims=True) / normalizer


def solution(mesh):
    in_specs = (
        P("section", "dp", "mp"),
        P("section", "dp", "mp"),
        P("section", "mp", None),
        P("section", "mp", None),
        P("section", None, "dp", "mp"),
        P("section", "dp", None, "mp"),
        P("section", "dp", None, "mp"),
        P(),
    )
    return jax.shard_map(
        per_device, mesh=mesh, in_specs=in_specs, out_specs=P("dp", None), check_vma=False
    )
```

```python
import functools
import math

import jax
import jax.numpy as jnp
from jax import lax
from jax.experimental import pallas as pl
from jax.experimental.pallas import tpu as pltpu
from jax.sharding import PartitionSpec as P

SEQLEN = 128
DAMPING = 0.1
ROWS = 16
CORES = 2
DEPTH = 4
MIB = 1 << 20


def tile_of(target, side):
    x, rest = divmod(target, DEPTH)
    z, core = divmod(rest, CORES)
    return (x * DEPTH + 2 * z + side) * CORES + core


def turn_acts_kernel(train_ref, query_ref, basis_ref, out_ref):
    rows = jnp.concatenate([train_ref[...], query_ref[...]], axis=0)
    out_ref[...] = jnp.dot(
        rows, basis_ref[...], preferred_element_type=jnp.float32
    ).astype(jnp.bfloat16)


def turn_grads_kernel(train_ref, query_ref, basis_ref, out_ref, turned, slots):
    step = pl.program_id(0)
    steps = pl.num_programs(0)
    size = basis_ref.shape[1]
    tokens = train_ref.shape[0]
    rows = jnp.concatenate([train_ref[...], query_ref[...]], axis=0)
    product = jnp.dot(rows, basis_ref[...], preferred_element_type=jnp.float32)
    turned[step] = product[:tokens].T.astype(jnp.bfloat16)
    slots[step] = product[tokens:]

    @pl.when(step == steps - 1)
    def _():
        targets, _, lanes = out_ref.shape
        total = turned.shape[0] * size
        piece = total // (2 * targets)
        length = slots.shape[1]
        for target in range(targets):
            for side in range(2):
                start = tile_of(target, side) * piece
                parts = []
                at = start
                while at < start + piece:
                    block = at // size
                    end = min(start + piece, (block + 1) * size)
                    parts.append(turned[block, at - block * size : end - block * size, :])
                    at = end
                rows = parts[0] if len(parts) == 1 else jnp.concatenate(parts, axis=0)
                out_ref[target, side * piece : (side + 1) * piece, :] = rows
                first = start // lanes
                tiles = []
                for tile in range(first, min(first + 2, total // lanes)):
                    col = tile * lanes
                    block = col // size
                    tiles.append(slots[block, :, col - block * size : col - block * size + lanes])
                window = jnp.concatenate(tiles, axis=1) if len(tiles) > 1 else tiles[0]
                shift = start - first * lanes
                if shift:
                    window = pltpu.roll(window, window.shape[1] - shift, 1)
                at = 2 * piece + side * length
                out_ref[target, at : at + length, :] = window[:, :lanes].astype(jnp.bfloat16)


def grams_of(step, steps, place_ref, part_refs, near_ref, far_ref, grams):
    blocks = grams.shape[0]
    pairs = near_ref.shape[1]
    for far, acts_ref in enumerate((near_ref, far_ref)):
        for n in range(pairs):
            place = place_ref[(far * steps + step) * pairs + n]
            inner = lax.rem(place, CORES * pairs)
            grads = jnp.concatenate([part[0, inner] for part in part_refs], axis=0)
            gram = jnp.dot(grads, acts_ref[0, n], preferred_element_type=jnp.float32)
            gram = gram.astype(jnp.bfloat16)
            start = pl.multiple_of(place * ROWS, ROWS)
            for b in range(blocks):
                grams[b, pl.ds(start, ROWS), :] = gram[b * ROWS : (b + 1) * ROWS]


def scores_of(grams, weighted, totals, out_ref):
    totals[...] = jnp.zeros_like(totals)
    group = 7

    @pl.loop(0, grams.shape[0] // group)
    def _(g):
        for b in range(group):
            totals[...] += lax.dot_general(
                grams[g * group + b],
                weighted[g * group + b],
                (((1,), (1,)), ((), ())),
                preferred_element_type=jnp.float32,
            )

    shape = totals.shape
    same = (
        lax.broadcasted_iota(jnp.int32, shape, 0) % ROWS
        == lax.broadcasted_iota(jnp.int32, shape, 1) % ROWS
    )
    kept = jnp.where(same, totals[...], 0.0)
    out_ref[...] = jnp.sum(kept.reshape(-1, ROWS, shape[1]), axis=1)


def first_kernel(length, order_ref, place_ref, *refs):
    (query_ref, query_acts_ref, own_ref, other_ref), refs = refs[:4], refs[4:]
    part_refs, refs = refs[:-7], refs[-7:]
    near_ref, far_ref, out_ref, last_ref, grams, weighted, totals = refs
    step = pl.program_id(0)
    steps = pl.num_programs(0)
    queries = query_acts_ref.shape[0] // length
    turned = query_ref[0].astype(jnp.float32).T
    shape = (queries * ROWS, queries * length)
    own = (
        lax.broadcasted_iota(jnp.int32, shape, 0) // ROWS
        == lax.broadcasted_iota(jnp.int32, shape, 1) // length
    )
    blocks = own_ref.shape[1] // ROWS
    lanes = query_ref.shape[2] // 2
    side_of_own = place_ref[4 * steps]
    for side in range(2):
        mine = side_of_own == side
        for b in range(blocks):
            rows = slice(b * ROWS, (b + 1) * ROWS)
            part = turned[side * lanes + b * ROWS : side * lanes + (b + 1) * ROWS]
            spread = jnp.concatenate([part] * queries, axis=0)
            spread = jnp.where(own, spread, 0.0).astype(jnp.bfloat16)
            moments = jnp.dot(spread, query_acts_ref[...], preferred_element_type=jnp.float32)
            values = jnp.where(mine, own_ref[0, rows, :], other_ref[0, rows, :].astype(jnp.float32))
            inverse = 1.0 / (values + DAMPING)
            moments = moments.reshape(queries, ROWS, moments.shape[1]) * inverse[None]
            moments = moments.reshape(queries * ROWS, moments.shape[2]).astype(jnp.bfloat16)
            weighted[step * (2 * blocks) + side * blocks + b] = moments

    grams_of(step, steps, place_ref, part_refs, near_ref, far_ref, grams)

    @pl.when(step == steps - 1)
    def _():
        last_ref[...] = weighted[(steps - 1) * 2 * blocks :]
        scores_of(grams, weighted, totals, out_ref)


def last_kernel(place_ref, low_ref, high_ref, near_ref, far_ref, weighted_ref, out_ref, grams, totals):
    step = pl.program_id(0)
    steps = pl.num_programs(0)
    grams_of(step, steps, place_ref, [low_ref, high_ref], near_ref, far_ref, grams)

    @pl.when(step == steps - 1)
    def _():
        scores_of(grams, weighted_ref, totals, out_ref)


def per_device(
    train_acts, train_grads, basis_in, basis_out, eigen_values, query_acts, query_grads, query_owner
):
    block_size = basis_in.shape[2]
    tokens, act_cols = train_acts.shape[1:]
    grad_cols = train_grads.shape[2]
    length = query_acts.shape[2]
    queries = query_owner.shape[0]
    data_size = lax.axis_size("dp")
    model_size = lax.axis_size("mp")
    piece = grad_cols // data_size
    bf16 = jnp.bfloat16

    turned_acts = pl.pallas_call(
        turn_acts_kernel,
        grid=(act_cols // block_size,),
        in_specs=[
            pl.BlockSpec((tokens, block_size), lambda s: (0, s)),
            pl.BlockSpec((length, block_size), lambda s: (0, s)),
            pl.BlockSpec((block_size, block_size), lambda s: (s, 0)),
        ],
        out_specs=pl.BlockSpec((tokens + length, block_size), lambda s: (0, s)),
        out_shape=jax.ShapeDtypeStruct((tokens + length, act_cols), bf16),
        compiler_params=pltpu.CompilerParams(vmem_limit_bytes=60 * MIB),
        name="turn_acts",
    )(train_acts[0], query_acts[0, 0], basis_in[0])
    width = data_size // (DEPTH * CORES)
    targets = data_size // 2
    classes = [[tile_of(t, parity) for t in range(targets)] for parity in range(2)]
    where = [(x, z, c) for x in range(width) for z in range(DEPTH) for c in range(CORES)]

    def shifted(dx=0, dz=0, flip_z=0, flip_c=0):
        at = lambda x, z, c: (x % width * DEPTH + z % DEPTH) * CORES + c
        return [
            (at(x, z, c), at(x + dx, (z + dz) % DEPTH ^ flip_z, c ^ flip_c)) for x, z, c in where
        ]

    data_index = lax.axis_index("dp")
    my_x = data_index // (DEPTH * CORES)
    my_z = data_index // CORES % DEPTH
    my_core = data_index % CORES
    my_class = my_z % 2

    other_values = lax.ppermute(eigen_values[0].astype(bf16), "dp", shifted(flip_z=1))

    other_acts = lax.ppermute(turned_acts, "dp", shifted(dz=2))

    steps = grad_cols // block_size
    rows = 2 * (piece + length)
    pieces = pl.pallas_call(
        turn_grads_kernel,
        grid=(steps,),
        in_specs=[
            pl.BlockSpec((tokens, block_size), lambda s: (0, s)),
            pl.BlockSpec((length, block_size), lambda s: (0, s)),
            pl.BlockSpec((block_size, block_size), lambda s: (s, 0)),
        ],
        out_specs=pl.BlockSpec((targets, rows, tokens), lambda s: (0, 0, 0)),
        out_shape=jax.ShapeDtypeStruct((targets, rows, tokens), bf16),
        scratch_shapes=[
            pltpu.VMEM((steps, block_size, tokens), bf16),
            pltpu.VMEM((steps, length, block_size), jnp.float32),
        ],
        compiler_params=pltpu.CompilerParams(vmem_limit_bytes=60 * MIB),
        name="turn_grads",
    )(train_grads[0], query_grads[0, 0], basis_out[0])
    turned_acts, other_acts, pieces = lax.optimization_barrier((turned_acts, other_acts, pieces))
    pair = jnp.stack([turned_acts, other_acts])
    moved = lax.all_to_all(
        pieces, "dp", split_axis=0, concat_axis=0, tiled=True, axis_index_groups=classes
    )
    others_x = [lax.ppermute(pair, "dp", shifted(dx=s)) for s in range(1, width)]
    moved, other_values, pair, *others_x = lax.optimization_barrier(
        (moved, other_values, pair, *others_x)
    )
    near = jnp.stack([pair] + others_x)
    own_grads = moved[:, : 2 * piece].reshape(width, DEPTH // 2 * CORES, 2 * piece, tokens)

    owner_x = query_owner // (DEPTH * CORES)
    owner_z = query_owner // CORES % DEPTH
    owner_core = query_owner % CORES
    in_class = (owner_z % 2 == my_class)[:, None, None]
    owner_place = (owner_x * (DEPTH // 2) + owner_z // 2) * CORES + owner_core
    chosen = jnp.take(moved[:, 2 * piece :], owner_place, axis=0)
    chosen = jnp.where(in_class, chosen, 0).astype(bf16)
    chosen = chosen.reshape(queries, 2, length, tokens).transpose(0, 2, 1, 3)
    chosen = chosen.reshape(queries * length, 2 * tokens)
    own_query = chosen + lax.ppermute(chosen, "dp", shifted(flip_z=1))

    ring = range(model_size)
    shifts = [[(i, (i + s) % model_size) for i in ring] for s in (1, model_size - 1, 2)]
    grad_parts = [own_grads] + [lax.ppermute(own_grads, "mp", pairs) for pairs in shifts[:2]]
    opposite = [
        lax.ppermute(grad_parts[1][:, :, :piece], "mp", shifts[0]),
        lax.ppermute(grad_parts[2][:, :, piece:], "mp", shifts[1]),
    ]
    own_query = jnp.broadcast_to(own_query[None], (model_size,) + own_query.shape)
    query_parts = lax.all_to_all(own_query, "mp", split_axis=0, concat_axis=0, tiled=True)
    model_index = lax.axis_index("mp")
    order = jnp.stack([(model_index + s) % model_size for s in (0, model_size - 1, 1, 2)])
    order = order.astype(jnp.int32)

    far = lax.ppermute(near, "dp", shifted(flip_c=1))
    places = [
        ((my_x + width - s) % width * (DEPTH // 2) + (my_z // 2 + n) % 2) * CORES
        + (my_core + flip) % CORES
        for flip in range(2)
        for s in range(width)
        for n in range(2)
    ]
    place = jnp.stack(places + [my_class]).astype(jnp.int32)

    slots = jnp.concatenate([near[:, :, tokens:], far[:, :, tokens:]], axis=0)
    slots = slots.reshape(CORES * width * 2, length, act_cols)
    relative = (owner_core ^ my_core) * width + (my_x + width - owner_x) % width
    relative = relative * 2 + (owner_z // 2 ^ my_z // 2)
    chosen_acts = jnp.where(in_class, jnp.take(slots, relative, axis=0), 0).astype(bf16)
    _, chosen_acts = lax.optimization_barrier((own_query, chosen_acts))
    chosen_acts = chosen_acts.reshape(queries * length, act_cols)
    chosen_acts = chosen_acts + lax.ppermute(chosen_acts, "dp", shifted(flip_z=1))

    blocks = piece // ROWS
    early = model_size - 1
    part_block = (1,) + own_grads.shape[1:]
    half_block = (1,) + opposite[0].shape[1:]
    acts_block = (1, 2, tokens, act_cols)
    weighted_shape = (2 * blocks, queries * ROWS, act_cols)
    total_shape = (targets * ROWS, queries * ROWS)
    score_shape = jax.ShapeDtypeStruct((targets, queries * ROWS), jnp.float32)

    def x_of(place, s):
        return lax.div(place[2 * s], DEPTH // 2 * CORES)

    work = 4 * targets * tokens * 2 * piece * act_cols
    early_scores, last_weighted = pl.pallas_call(
        functools.partial(first_kernel, length),
        grid_spec=pltpu.PrefetchScalarGridSpec(
            num_scalar_prefetch=2,
            grid=(width,),
            in_specs=[
                pl.BlockSpec(
                    (1, queries * length, 2 * tokens), lambda s, order, place: (order[s], 0, 0)
                ),
                pl.BlockSpec((queries * length, act_cols), lambda s, order, place: (0, 0)),
                pl.BlockSpec((1, piece, act_cols), lambda s, order, place: (order[s], 0, 0)),
                pl.BlockSpec((1, piece, act_cols), lambda s, order, place: (order[s], 0, 0)),
            ]
            + [pl.BlockSpec(part_block, lambda s, order, place: (x_of(place, s), 0, 0, 0))] * early
            + [pl.BlockSpec(acts_block, lambda s, order, place: (s, 0, 0, 0))] * 2,
            out_specs=[
                pl.BlockSpec(score_shape.shape, lambda s, order, place: (0, 0)),
                pl.BlockSpec(weighted_shape, lambda s, order, place: (0, 0, 0)),
            ],
            scratch_shapes=[
                pltpu.VMEM((early * 2 * blocks, targets * ROWS, act_cols), bf16),
                pltpu.VMEM((model_size * 2 * blocks,) + weighted_shape[1:], bf16),
                pltpu.VMEM(total_shape, jnp.float32),
            ],
        ),
        out_shape=[score_shape, jax.ShapeDtypeStruct(weighted_shape, bf16)],
        compiler_params=pltpu.CompilerParams(vmem_limit_bytes=60 * MIB),
        cost_estimate=pl.CostEstimate(flops=early * work, bytes_accessed=16 * MIB, transcendentals=0),
        name="first_scores",
    )(order, place, query_parts, chosen_acts, eigen_values[0], other_values,
      *grad_parts[:early], near, far)
    last_scores = pl.pallas_call(
        last_kernel,
        grid_spec=pltpu.PrefetchScalarGridSpec(
            num_scalar_prefetch=1,
            grid=(width,),
            in_specs=[
                *[pl.BlockSpec(half_block, lambda s, place: (x_of(place, s), 0, 0, 0))] * 2,
                pl.BlockSpec(acts_block, lambda s, place: (s, 0, 0, 0)),
                pl.BlockSpec(acts_block, lambda s, place: (s, 0, 0, 0)),
                pl.BlockSpec(weighted_shape, lambda s, place: (0, 0, 0)),
            ],
            out_specs=pl.BlockSpec(score_shape.shape, lambda s, place: (0, 0)),
            scratch_shapes=[
                pltpu.VMEM((2 * blocks, targets * ROWS, act_cols), bf16),
                pltpu.VMEM(total_shape, jnp.float32),
            ],
        ),
        out_shape=score_shape,
        compiler_params=pltpu.CompilerParams(vmem_limit_bytes=60 * MIB),
        cost_estimate=pl.CostEstimate(flops=work, bytes_accessed=9 * MIB, transcendentals=0),
        name="last_scores",
    )(place, *opposite, near, far, last_weighted)
    scores = early_scores + last_scores
    partial = scores.reshape(targets, queries, ROWS).sum(axis=2)

    mine = lax.all_to_all(
        partial, "dp", split_axis=0, concat_axis=0, tiled=True, axis_index_groups=classes
    ).sum(axis=0)
    others = model_size * lax.axis_size("section")
    spread = jnp.broadcast_to(mine[None], (others, queries))
    gathered = lax.all_to_all(spread, ("section", "mp"), split_axis=0, concat_axis=0, tiled=True)
    layers = train_acts.shape[0] * lax.axis_size("section")
    normalizer = math.sqrt(
        layers * act_cols * model_size * grad_cols * model_size * SEQLEN * length
    )
    return gathered.sum(axis=0, keepdims=True) / normalizer


def solution(mesh):
    in_specs = (
        P("section", "dp", "mp"),
        P("section", "dp", "mp"),
        P("section", "mp", None),
        P("section", "mp", None),
        P("section", None, "dp", "mp"),
        P("section", "dp", None, "mp"),
        P("section", "dp", None, "mp"),
        P(),
    )
    return jax.shard_map(
        per_device, mesh=mesh, in_specs=in_specs, out_specs=P("dp", None), check_vma=False
    )
```

```python
import functools
import math

import jax
import jax.numpy as jnp
from jax import lax
from jax.experimental import pallas as pl
from jax.experimental.pallas import tpu as pltpu
from jax.sharding import PartitionSpec as P

SEQLEN = 128
DAMPING = 0.1
ROWS = 16
CORES = 2
DEPTH = 4
MIB = 1 << 20


def tile_of(target, side):
    x, rest = divmod(target, DEPTH)
    z, core = divmod(rest, CORES)
    return (x * DEPTH + 2 * z + side) * CORES + core


def turn_acts_kernel(train_ref, query_ref, basis_ref, out_ref):
    rows = jnp.concatenate([train_ref[...], query_ref[...]], axis=0)
    out_ref[...] = jnp.dot(
        rows, basis_ref[...], preferred_element_type=jnp.float32
    ).astype(jnp.bfloat16)


def turn_grads_kernel(train_ref, query_ref, basis_ref, out_ref, turned, slots):
    step = pl.program_id(0)
    steps = pl.num_programs(0)
    size = basis_ref.shape[1]
    tokens = train_ref.shape[0]
    rows = jnp.concatenate([train_ref[...], query_ref[...]], axis=0)
    product = jnp.dot(rows, basis_ref[...], preferred_element_type=jnp.float32)
    turned[step] = product[:tokens].T.astype(jnp.bfloat16)
    slots[step] = product[tokens:]

    @pl.when(step == steps - 1)
    def _():
        targets, _, lanes = out_ref.shape
        total = turned.shape[0] * size
        piece = total // (2 * targets)
        length = slots.shape[1]
        for target in range(targets):
            for side in range(2):
                start = tile_of(target, side) * piece
                parts = []
                at = start
                while at < start + piece:
                    block = at // size
                    end = min(start + piece, (block + 1) * size)
                    parts.append(turned[block, at - block * size : end - block * size, :])
                    at = end
                rows = parts[0] if len(parts) == 1 else jnp.concatenate(parts, axis=0)
                out_ref[target, side * piece : (side + 1) * piece, :] = rows
                first = start // lanes
                tiles = []
                for tile in range(first, min(first + 2, total // lanes)):
                    col = tile * lanes
                    block = col // size
                    tiles.append(slots[block, :, col - block * size : col - block * size + lanes])
                window = jnp.concatenate(tiles, axis=1) if len(tiles) > 1 else tiles[0]
                shift = start - first * lanes
                if shift:
                    window = pltpu.roll(window, window.shape[1] - shift, 1)
                at = 2 * piece + side * length
                out_ref[target, at : at + length, :] = window[:, :lanes].astype(jnp.bfloat16)


def grams_of(step, steps, place_ref, part_refs, near_ref, far_ref, grams):
    blocks = grams.shape[0]
    pairs = near_ref.shape[1]
    for far, acts_ref in enumerate((near_ref, far_ref)):
        for n in range(pairs):
            place = place_ref[(far * steps + step) * pairs + n]
            inner = lax.rem(place, CORES * pairs)
            grads = jnp.concatenate([part[0, inner] for part in part_refs], axis=0)
            gram = jnp.dot(grads, acts_ref[0, n], preferred_element_type=jnp.float32)
            gram = gram.astype(jnp.bfloat16)
            start = pl.multiple_of(place * ROWS, ROWS)
            for b in range(blocks):
                grams[b, pl.ds(start, ROWS), :] = gram[b * ROWS : (b + 1) * ROWS]


def scores_of(grams, weighted, totals, out_ref):
    totals[...] = jnp.zeros_like(totals)
    group = 7

    @pl.loop(0, grams.shape[0] // group)
    def _(g):
        for b in range(group):
            totals[...] += lax.dot_general(
                grams[g * group + b],
                weighted[g * group + b],
                (((1,), (1,)), ((), ())),
                preferred_element_type=jnp.float32,
            )

    shape = totals.shape
    same = (
        lax.broadcasted_iota(jnp.int32, shape, 0) % ROWS
        == lax.broadcasted_iota(jnp.int32, shape, 1) % ROWS
    )
    kept = jnp.where(same, totals[...], 0.0)
    out_ref[...] = jnp.sum(kept.reshape(-1, ROWS, shape[1]), axis=1)


def first_kernel(length, order_ref, place_ref, *refs):
    (query_ref, query_acts_ref, own_ref, other_ref), refs = refs[:4], refs[4:]
    part_refs, refs = refs[:-7], refs[-7:]
    near_ref, far_ref, out_ref, last_ref, grams, weighted, totals = refs
    step = pl.program_id(0)
    steps = pl.num_programs(0)
    queries = query_acts_ref.shape[0] // length
    turned = query_ref[0].astype(jnp.float32).T
    shape = (queries * ROWS, queries * length)
    own = (
        lax.broadcasted_iota(jnp.int32, shape, 0) // ROWS
        == lax.broadcasted_iota(jnp.int32, shape, 1) // length
    )
    blocks = own_ref.shape[1] // ROWS
    lanes = query_ref.shape[2] // 2
    side_of_own = place_ref[4 * steps]
    for side in range(2):
        mine = side_of_own == side
        for b in range(blocks):
            rows = slice(b * ROWS, (b + 1) * ROWS)
            part = turned[side * lanes + b * ROWS : side * lanes + (b + 1) * ROWS]
            spread = jnp.concatenate([part] * queries, axis=0)
            spread = jnp.where(own, spread, 0.0).astype(jnp.bfloat16)
            moments = jnp.dot(spread, query_acts_ref[...], preferred_element_type=jnp.float32)
            values = jnp.where(mine, own_ref[0, rows, :], other_ref[0, rows, :].astype(jnp.float32))
            inverse = 1.0 / (values + DAMPING)
            moments = moments.reshape(queries, ROWS, moments.shape[1]) * inverse[None]
            moments = moments.reshape(queries * ROWS, moments.shape[2]).astype(jnp.bfloat16)
            weighted[step * (2 * blocks) + side * blocks + b] = moments

    grams_of(step, steps, place_ref, part_refs, near_ref, far_ref, grams)

    @pl.when(step == steps - 1)
    def _():
        last_ref[...] = weighted[(steps - 1) * 2 * blocks :]
        scores_of(grams, weighted, totals, out_ref)


def last_kernel(place_ref, low_ref, high_ref, near_ref, far_ref, weighted_ref, out_ref, grams, totals):
    step = pl.program_id(0)
    steps = pl.num_programs(0)
    grams_of(step, steps, place_ref, [low_ref, high_ref], near_ref, far_ref, grams)

    @pl.when(step == steps - 1)
    def _():
        scores_of(grams, weighted_ref, totals, out_ref)


def per_device(
    train_acts, train_grads, basis_in, basis_out, eigen_values, query_acts, query_grads, query_owner
):
    block_size = basis_in.shape[2]
    tokens, act_cols = train_acts.shape[1:]
    grad_cols = train_grads.shape[2]
    length = query_acts.shape[2]
    queries = query_owner.shape[0]
    data_size = lax.axis_size("dp")
    model_size = lax.axis_size("mp")
    piece = grad_cols // data_size
    bf16 = jnp.bfloat16

    turned_acts = pl.pallas_call(
        turn_acts_kernel,
        grid=(act_cols // block_size,),
        in_specs=[
            pl.BlockSpec((tokens, block_size), lambda s: (0, s)),
            pl.BlockSpec((length, block_size), lambda s: (0, s)),
            pl.BlockSpec((block_size, block_size), lambda s: (s, 0)),
        ],
        out_specs=pl.BlockSpec((tokens + length, block_size), lambda s: (0, s)),
        out_shape=jax.ShapeDtypeStruct((tokens + length, act_cols), bf16),
        compiler_params=pltpu.CompilerParams(vmem_limit_bytes=60 * MIB),
        name="turn_acts",
    )(train_acts[0], query_acts[0, 0], basis_in[0])
    width = data_size // (DEPTH * CORES)
    targets = data_size // 2
    classes = [[tile_of(t, parity) for t in range(targets)] for parity in range(2)]
    where = [(x, z, c) for x in range(width) for z in range(DEPTH) for c in range(CORES)]

    def shifted(dx=0, dz=0, flip_z=0, flip_c=0):
        at = lambda x, z, c: (x % width * DEPTH + z % DEPTH) * CORES + c
        return [
            (at(x, z, c), at(x + dx, (z + dz) % DEPTH ^ flip_z, c ^ flip_c)) for x, z, c in where
        ]

    data_index = lax.axis_index("dp")
    my_x = data_index // (DEPTH * CORES)
    my_z = data_index // CORES % DEPTH
    my_core = data_index % CORES
    my_class = my_z % 2

    other_values = lax.ppermute(eigen_values[0].astype(bf16), "dp", shifted(flip_z=1))

    other_acts = lax.ppermute(turned_acts, "dp", shifted(dz=2))

    steps = grad_cols // block_size
    rows = 2 * (piece + length)
    pieces = pl.pallas_call(
        turn_grads_kernel,
        grid=(steps,),
        in_specs=[
            pl.BlockSpec((tokens, block_size), lambda s: (0, s)),
            pl.BlockSpec((length, block_size), lambda s: (0, s)),
            pl.BlockSpec((block_size, block_size), lambda s: (s, 0)),
        ],
        out_specs=pl.BlockSpec((targets, rows, tokens), lambda s: (0, 0, 0)),
        out_shape=jax.ShapeDtypeStruct((targets, rows, tokens), bf16),
        scratch_shapes=[
            pltpu.VMEM((steps, block_size, tokens), bf16),
            pltpu.VMEM((steps, length, block_size), jnp.float32),
        ],
        compiler_params=pltpu.CompilerParams(vmem_limit_bytes=60 * MIB),
        name="turn_grads",
    )(train_grads[0], query_grads[0, 0], basis_out[0])
    turned_acts, other_acts, pieces = lax.optimization_barrier((turned_acts, other_acts, pieces))
    pair = jnp.stack([turned_acts, other_acts])
    moved = lax.all_to_all(
        pieces, "dp", split_axis=0, concat_axis=0, tiled=True, axis_index_groups=classes
    )
    others_x = [lax.ppermute(pair, "dp", shifted(dx=s)) for s in range(1, width)]
    moved, other_values, pair, *others_x = lax.optimization_barrier(
        (moved, other_values, pair, *others_x)
    )
    near = jnp.stack([pair] + others_x)
    own_grads = moved[:, : 2 * piece].reshape(width, DEPTH // 2 * CORES, 2 * piece, tokens)

    owner_x = query_owner // (DEPTH * CORES)
    owner_z = query_owner // CORES % DEPTH
    owner_core = query_owner % CORES
    in_class = (owner_z % 2 == my_class)[:, None, None]
    owner_place = (owner_x * (DEPTH // 2) + owner_z // 2) * CORES + owner_core
    chosen = jnp.take(moved[:, 2 * piece :], owner_place, axis=0)
    chosen = jnp.where(in_class, chosen, 0).astype(bf16)
    chosen = chosen.reshape(queries, 2, length, tokens).transpose(0, 2, 1, 3)
    chosen = chosen.reshape(queries * length, 2 * tokens)
    own_query = chosen + lax.ppermute(chosen, "dp", shifted(flip_z=1))

    ring = range(model_size)
    shifts = [[(i, (i + s) % model_size) for i in ring] for s in (1, model_size - 1, 2)]
    grad_parts = [own_grads] + [lax.ppermute(own_grads, "mp", pairs) for pairs in shifts[:2]]
    opposite = [
        lax.ppermute(grad_parts[1][:, :, :piece], "mp", shifts[0]),
        lax.ppermute(grad_parts[2][:, :, piece:], "mp", shifts[1]),
    ]
    own_query = jnp.broadcast_to(own_query[None], (model_size,) + own_query.shape)
    query_parts = lax.all_to_all(own_query, "mp", split_axis=0, concat_axis=0, tiled=True)
    model_index = lax.axis_index("mp")
    order = jnp.stack([(model_index + s) % model_size for s in (0, model_size - 1, 1, 2)])
    order = order.astype(jnp.int32)

    far = lax.ppermute(near, "dp", shifted(flip_c=1))
    places = [
        ((my_x + width - s) % width * (DEPTH // 2) + (my_z // 2 + n) % 2) * CORES
        + (my_core + flip) % CORES
        for flip in range(2)
        for s in range(width)
        for n in range(2)
    ]
    place = jnp.stack(places + [my_class]).astype(jnp.int32)

    slots = jnp.concatenate([near[:, :, tokens:], far[:, :, tokens:]], axis=0)
    slots = slots.reshape(CORES * width * 2, length, act_cols)
    relative = (owner_core ^ my_core) * width + (my_x + width - owner_x) % width
    relative = relative * 2 + (owner_z // 2 ^ my_z // 2)
    chosen_acts = jnp.where(in_class, jnp.take(slots, relative, axis=0), 0).astype(bf16)
    _, chosen_acts = lax.optimization_barrier((own_query, chosen_acts))
    chosen_acts = chosen_acts.reshape(queries * length, act_cols)
    chosen_acts = chosen_acts + lax.ppermute(chosen_acts, "dp", shifted(flip_z=1))

    blocks = piece // ROWS
    early = model_size - 1
    part_block = (1,) + own_grads.shape[1:]
    half_block = (1,) + opposite[0].shape[1:]
    acts_block = (1, 2, tokens, act_cols)
    weighted_shape = (2 * blocks, queries * ROWS, act_cols)
    total_shape = (targets * ROWS, queries * ROWS)
    score_shape = jax.ShapeDtypeStruct((targets, queries * ROWS), jnp.float32)

    def x_of(place, s):
        return lax.div(place[2 * s], DEPTH // 2 * CORES)

    work = 4 * targets * tokens * 2 * piece * act_cols
    early_scores, last_weighted = pl.pallas_call(
        functools.partial(first_kernel, length),
        grid_spec=pltpu.PrefetchScalarGridSpec(
            num_scalar_prefetch=2,
            grid=(width,),
            in_specs=[
                pl.BlockSpec(
                    (1, queries * length, 2 * tokens), lambda s, order, place: (order[s], 0, 0)
                ),
                pl.BlockSpec((queries * length, act_cols), lambda s, order, place: (0, 0)),
                pl.BlockSpec((1, piece, act_cols), lambda s, order, place: (order[s], 0, 0)),
                pl.BlockSpec((1, piece, act_cols), lambda s, order, place: (order[s], 0, 0)),
            ]
            + [pl.BlockSpec(part_block, lambda s, order, place: (x_of(place, s), 0, 0, 0))] * early
            + [pl.BlockSpec(acts_block, lambda s, order, place: (s, 0, 0, 0))] * 2,
            out_specs=[
                pl.BlockSpec(score_shape.shape, lambda s, order, place: (0, 0)),
                pl.BlockSpec(weighted_shape, lambda s, order, place: (0, 0, 0)),
            ],
            scratch_shapes=[
                pltpu.VMEM((early * 2 * blocks, targets * ROWS, act_cols), bf16),
                pltpu.VMEM((model_size * 2 * blocks,) + weighted_shape[1:], bf16),
                pltpu.VMEM(total_shape, jnp.float32),
            ],
        ),
        out_shape=[score_shape, jax.ShapeDtypeStruct(weighted_shape, bf16)],
        compiler_params=pltpu.CompilerParams(vmem_limit_bytes=60 * MIB),
        cost_estimate=pl.CostEstimate(flops=early * work, bytes_accessed=16 * MIB, transcendentals=0),
        name="first_scores",
    )(order, place, query_parts, chosen_acts, eigen_values[0], other_values,
      *grad_parts[:early], near, far)
    last_scores = pl.pallas_call(
        last_kernel,
        grid_spec=pltpu.PrefetchScalarGridSpec(
            num_scalar_prefetch=1,
            grid=(width,),
            in_specs=[
                *[pl.BlockSpec(half_block, lambda s, place: (x_of(place, s), 0, 0, 0))] * 2,
                pl.BlockSpec(acts_block, lambda s, place: (s, 0, 0, 0)),
                pl.BlockSpec(acts_block, lambda s, place: (s, 0, 0, 0)),
                pl.BlockSpec(weighted_shape, lambda s, place: (0, 0, 0)),
            ],
            out_specs=pl.BlockSpec(score_shape.shape, lambda s, place: (0, 0)),
            scratch_shapes=[
                pltpu.VMEM((2 * blocks, targets * ROWS, act_cols), bf16),
                pltpu.VMEM(total_shape, jnp.float32),
            ],
        ),
        out_shape=score_shape,
        compiler_params=pltpu.CompilerParams(vmem_limit_bytes=60 * MIB),
        cost_estimate=pl.CostEstimate(flops=work, bytes_accessed=9 * MIB, transcendentals=0),
        name="last_scores",
    )(place, *opposite, near, far, last_weighted)
    scores = early_scores + last_scores
    partial = scores.reshape(targets, queries, ROWS).sum(axis=2)

    rows = partial.reshape(width, DEPTH // 2, 1, CORES, queries)
    parities = jnp.arange(2).reshape(1, 1, 2, 1, 1)
    rows = jnp.where(parities == my_class, rows, 0.0).reshape(data_size, 1, queries)
    rows = jnp.broadcast_to(rows, (data_size, model_size, queries))
    rows = rows.reshape(data_size * model_size, queries)
    rows = lax.all_to_all(rows, ("dp", "mp"), split_axis=0, concat_axis=0, tiled=True)
    mine = rows.sum(axis=0, keepdims=True)
    sections = lax.axis_size("section")
    swapped = [(i, (i + 1) % sections) for i in range(sections)]
    mine = mine + lax.ppermute(mine, "section", swapped)
    layers = train_acts.shape[0] * lax.axis_size("section")
    normalizer = math.sqrt(
        layers * act_cols * model_size * grad_cols * model_size * SEQLEN * length
    )
    return mine / normalizer


def solution(mesh):
    in_specs = (
        P("section", "dp", "mp"),
        P("section", "dp", "mp"),
        P("section", "mp", None),
        P("section", "mp", None),
        P("section", None, "dp", "mp"),
        P("section", "dp", None, "mp"),
        P("section", "dp", None, "mp"),
        P(),
    )
    return jax.shard_map(
        per_device, mesh=mesh, in_specs=in_specs, out_specs=P("dp", None), check_vma=False
    )
```

```python
import functools
import math

import jax
import jax.numpy as jnp
from jax import lax
from jax.experimental import pallas as pl
from jax.experimental.pallas import tpu as pltpu
from jax.sharding import PartitionSpec as P

SEQLEN = 128
DAMPING = 0.1
ROWS = 16
CORES = 2
DEPTH = 4
MIB = 1 << 20


def tile_of(target, side):
    x, rest = divmod(target, DEPTH)
    z, core = divmod(rest, CORES)
    return (x * DEPTH + 2 * z + side) * CORES + core


def turn_acts_kernel(train_ref, query_ref, basis_ref, out_ref):
    rows = jnp.concatenate([train_ref[...], query_ref[...]], axis=0)
    out_ref[...] = jnp.dot(
        rows, basis_ref[...], preferred_element_type=jnp.float32
    ).astype(jnp.bfloat16)


def turn_grads_kernel(train_ref, query_ref, basis_ref, out_ref, turned, slots):
    step = pl.program_id(0)
    steps = pl.num_programs(0)
    size = basis_ref.shape[1]
    tokens = train_ref.shape[0]
    rows = jnp.concatenate([train_ref[...], query_ref[...]], axis=0)
    product = jnp.dot(rows, basis_ref[...], preferred_element_type=jnp.float32)
    turned[step] = product[:tokens].T.astype(jnp.bfloat16)
    slots[step] = product[tokens:]

    @pl.when(step == steps - 1)
    def _():
        targets, _, lanes = out_ref.shape
        total = turned.shape[0] * size
        piece = total // (2 * targets)
        length = slots.shape[1]
        for target in range(targets):
            for side in range(2):
                start = tile_of(target, side) * piece
                parts = []
                at = start
                while at < start + piece:
                    block = at // size
                    end = min(start + piece, (block + 1) * size)
                    parts.append(turned[block, at - block * size : end - block * size, :])
                    at = end
                rows = parts[0] if len(parts) == 1 else jnp.concatenate(parts, axis=0)
                out_ref[target, side * piece : (side + 1) * piece, :] = rows
                first = start // lanes
                tiles = []
                for tile in range(first, min(first + 2, total // lanes)):
                    col = tile * lanes
                    block = col // size
                    tiles.append(slots[block, :, col - block * size : col - block * size + lanes])
                window = jnp.concatenate(tiles, axis=1) if len(tiles) > 1 else tiles[0]
                shift = start - first * lanes
                if shift:
                    window = pltpu.roll(window, window.shape[1] - shift, 1)
                at = 2 * piece + side * length
                out_ref[target, at : at + length, :] = window[:, :lanes].astype(jnp.bfloat16)


def grams_of(step, steps, place_ref, part_refs, near_ref, far_ref, grams):
    blocks = grams.shape[0]
    pairs = near_ref.shape[1]
    for far, acts_ref in enumerate((near_ref, far_ref)):
        for n in range(pairs):
            place = place_ref[(far * steps + step) * pairs + n]
            inner = lax.rem(place, CORES * pairs)
            grads = jnp.concatenate([part[0, inner] for part in part_refs], axis=0)
            gram = jnp.dot(grads, acts_ref[0, n], preferred_element_type=jnp.float32)
            gram = gram.astype(jnp.bfloat16)
            start = pl.multiple_of(place * ROWS, ROWS)
            for b in range(blocks):
                grams[b, pl.ds(start, ROWS), :] = gram[b * ROWS : (b + 1) * ROWS]


def scores_of(grams, weighted, totals, out_ref):
    totals[...] = jnp.zeros_like(totals)
    group = 7

    @pl.loop(0, grams.shape[0] // group)
    def _(g):
        for b in range(group):
            totals[...] += lax.dot_general(
                grams[g * group + b],
                weighted[g * group + b],
                (((1,), (1,)), ((), ())),
                preferred_element_type=jnp.float32,
            )

    shape = totals.shape
    same = (
        lax.broadcasted_iota(jnp.int32, shape, 0) % ROWS
        == lax.broadcasted_iota(jnp.int32, shape, 1) % ROWS
    )
    kept = jnp.where(same, totals[...], 0.0)
    out_ref[...] = jnp.sum(kept.reshape(-1, ROWS, shape[1]), axis=1)


def first_kernel(length, order_ref, place_ref, *refs):
    (query_ref, query_acts_ref, own_ref, other_ref), refs = refs[:4], refs[4:]
    part_refs, refs = refs[:-7], refs[-7:]
    near_ref, far_ref, out_ref, last_ref, grams, weighted, totals = refs
    step = pl.program_id(0)
    steps = pl.num_programs(0)
    queries = query_acts_ref.shape[0] // length
    turned = query_ref[0].astype(jnp.float32).T
    shape = (queries * ROWS, queries * length)
    own = (
        lax.broadcasted_iota(jnp.int32, shape, 0) // ROWS
        == lax.broadcasted_iota(jnp.int32, shape, 1) // length
    )
    blocks = own_ref.shape[1] // ROWS
    lanes = query_ref.shape[2] // 2
    side_of_own = place_ref[4 * steps]
    for side in range(2):
        mine = side_of_own == side
        for b in range(blocks):
            rows = slice(b * ROWS, (b + 1) * ROWS)
            part = turned[side * lanes + b * ROWS : side * lanes + (b + 1) * ROWS]
            spread = jnp.concatenate([part] * queries, axis=0)
            spread = jnp.where(own, spread, 0.0).astype(jnp.bfloat16)
            moments = jnp.dot(spread, query_acts_ref[...], preferred_element_type=jnp.float32)
            values = jnp.where(mine, own_ref[0, rows, :], other_ref[0, rows, :].astype(jnp.float32))
            inverse = 1.0 / (values + DAMPING)
            moments = moments.reshape(queries, ROWS, moments.shape[1]) * inverse[None]
            moments = moments.reshape(queries * ROWS, moments.shape[2]).astype(jnp.bfloat16)
            weighted[step * (2 * blocks) + side * blocks + b] = moments

    grams_of(step, steps, place_ref, part_refs, near_ref, far_ref, grams)

    @pl.when(step == steps - 1)
    def _():
        last_ref[...] = weighted[(steps - 1) * 2 * blocks :]
        scores_of(grams, weighted, totals, out_ref)


def last_kernel(
    place_ref, part_ref, near_ref, far_ref, weighted_ref, out_ref, grams, weighted, totals, arrived
):
    step = pl.program_id(0)
    steps = pl.num_programs(0)
    load = pltpu.make_async_copy(weighted_ref, weighted, arrived)

    @pl.when(step == 0)
    def _():
        load.start()

    grams_of(step, steps, place_ref, [part_ref], near_ref, far_ref, grams)

    @pl.when(step == steps - 1)
    def _():
        load.wait()
        scores_of(grams, weighted, totals, out_ref)


def per_device(
    train_acts, train_grads, basis_in, basis_out, eigen_values, query_acts, query_grads, query_owner
):
    block_size = basis_in.shape[2]
    tokens, act_cols = train_acts.shape[1:]
    grad_cols = train_grads.shape[2]
    length = query_acts.shape[2]
    queries = query_owner.shape[0]
    data_size = lax.axis_size("dp")
    model_size = lax.axis_size("mp")
    piece = grad_cols // data_size
    bf16 = jnp.bfloat16

    turned_acts = pl.pallas_call(
        turn_acts_kernel,
        grid=(act_cols // block_size,),
        in_specs=[
            pl.BlockSpec((tokens, block_size), lambda s: (0, s)),
            pl.BlockSpec((length, block_size), lambda s: (0, s)),
            pl.BlockSpec((block_size, block_size), lambda s: (s, 0)),
        ],
        out_specs=pl.BlockSpec((tokens + length, block_size), lambda s: (0, s)),
        out_shape=jax.ShapeDtypeStruct((tokens + length, act_cols), bf16),
        compiler_params=pltpu.CompilerParams(vmem_limit_bytes=60 * MIB),
        name="turn_acts",
    )(train_acts[0], query_acts[0, 0], basis_in[0])
    width = data_size // (DEPTH * CORES)
    targets = data_size // 2
    classes = [[tile_of(t, parity) for t in range(targets)] for parity in range(2)]
    where = [(x, z, c) for x in range(width) for z in range(DEPTH) for c in range(CORES)]

    def shifted(dx=0, dz=0, flip_z=0, flip_c=0):
        at = lambda x, z, c: (x % width * DEPTH + z % DEPTH) * CORES + c
        return [
            (at(x, z, c), at(x + dx, (z + dz) % DEPTH ^ flip_z, c ^ flip_c)) for x, z, c in where
        ]

    data_index = lax.axis_index("dp")
    my_x = data_index // (DEPTH * CORES)
    my_z = data_index // CORES % DEPTH
    my_core = data_index % CORES
    my_class = my_z % 2

    other_values = lax.ppermute(eigen_values[0].astype(bf16), "dp", shifted(flip_z=1))

    other_acts = lax.ppermute(turned_acts, "dp", shifted(dz=2))

    steps = grad_cols // block_size
    rows = 2 * (piece + length)
    pieces = pl.pallas_call(
        turn_grads_kernel,
        grid=(steps,),
        in_specs=[
            pl.BlockSpec((tokens, block_size), lambda s: (0, s)),
            pl.BlockSpec((length, block_size), lambda s: (0, s)),
            pl.BlockSpec((block_size, block_size), lambda s: (s, 0)),
        ],
        out_specs=pl.BlockSpec((targets, rows, tokens), lambda s: (0, 0, 0)),
        out_shape=jax.ShapeDtypeStruct((targets, rows, tokens), bf16),
        scratch_shapes=[
            pltpu.VMEM((steps, block_size, tokens), bf16),
            pltpu.VMEM((steps, length, block_size), jnp.float32),
        ],
        compiler_params=pltpu.CompilerParams(vmem_limit_bytes=60 * MIB),
        name="turn_grads",
    )(train_grads[0], query_grads[0, 0], basis_out[0])
    turned_acts, other_acts, pieces = lax.optimization_barrier((turned_acts, other_acts, pieces))
    pair = jnp.stack([turned_acts, other_acts])
    moved = lax.all_to_all(
        pieces, "dp", split_axis=0, concat_axis=0, tiled=True, axis_index_groups=classes
    )
    others_x = [lax.ppermute(pair, "dp", shifted(dx=s)) for s in range(1, width)]
    moved, other_values, pair, *others_x = lax.optimization_barrier(
        (moved, other_values, pair, *others_x)
    )
    near = jnp.stack([pair] + others_x)
    own_grads = moved[:, : 2 * piece].reshape(width, DEPTH // 2 * CORES, 2 * piece, tokens)

    owner_x = query_owner // (DEPTH * CORES)
    owner_z = query_owner // CORES % DEPTH
    owner_core = query_owner % CORES
    in_class = (owner_z % 2 == my_class)[:, None, None]
    owner_place = (owner_x * (DEPTH // 2) + owner_z // 2) * CORES + owner_core
    chosen = jnp.take(moved[:, 2 * piece :], owner_place, axis=0)
    chosen = jnp.where(in_class, chosen, 0).astype(bf16)
    chosen = chosen.reshape(queries, 2, length, tokens).transpose(0, 2, 1, 3)
    chosen = chosen.reshape(queries * length, 2 * tokens)
    own_query = chosen + lax.ppermute(chosen, "dp", shifted(flip_z=1))

    ring = range(model_size)
    shifts = [[(i, (i + s) % model_size) for i in ring] for s in (1, model_size - 1)]
    grad_parts = [own_grads] + [lax.ppermute(own_grads, "mp", pairs) for pairs in shifts]
    opposite = lax.ppermute(grad_parts[1], "mp", shifts[0])
    own_query = jnp.broadcast_to(own_query[None], (model_size,) + own_query.shape)
    query_parts = lax.all_to_all(own_query, "mp", split_axis=0, concat_axis=0, tiled=True)
    model_index = lax.axis_index("mp")
    order = jnp.stack([(model_index + s) % model_size for s in (0, model_size - 1, 1, 2)])
    order = order.astype(jnp.int32)

    far = lax.ppermute(near, "dp", shifted(flip_c=1))
    places = [
        ((my_x + width - s) % width * (DEPTH // 2) + (my_z // 2 + n) % 2) * CORES
        + (my_core + flip) % CORES
        for flip in range(2)
        for s in range(width)
        for n in range(2)
    ]
    place = jnp.stack(places + [my_class]).astype(jnp.int32)

    slots = jnp.concatenate([near[:, :, tokens:], far[:, :, tokens:]], axis=0)
    slots = slots.reshape(CORES * width * 2, length, act_cols)
    relative = (owner_core ^ my_core) * width + (my_x + width - owner_x) % width
    relative = relative * 2 + (owner_z // 2 ^ my_z // 2)
    chosen_acts = jnp.where(in_class, jnp.take(slots, relative, axis=0), 0).astype(bf16)
    _, chosen_acts = lax.optimization_barrier((own_query, chosen_acts))
    chosen_acts = chosen_acts.reshape(queries * length, act_cols)
    chosen_acts = chosen_acts + lax.ppermute(chosen_acts, "dp", shifted(flip_z=1))

    blocks = piece // ROWS
    early = model_size - 1
    part_block = (1,) + own_grads.shape[1:]
    acts_block = (1, 2, tokens, act_cols)
    weighted_shape = (2 * blocks, queries * ROWS, act_cols)
    total_shape = (targets * ROWS, queries * ROWS)
    score_shape = jax.ShapeDtypeStruct((targets, queries * ROWS), jnp.float32)

    def x_of(place, s):
        return lax.div(place[2 * s], DEPTH // 2 * CORES)

    work = 4 * targets * tokens * 2 * piece * act_cols
    early_scores, last_weighted = pl.pallas_call(
        functools.partial(first_kernel, length),
        grid_spec=pltpu.PrefetchScalarGridSpec(
            num_scalar_prefetch=2,
            grid=(width,),
            in_specs=[
                pl.BlockSpec(
                    (1, queries * length, 2 * tokens), lambda s, order, place: (order[s], 0, 0)
                ),
                pl.BlockSpec((queries * length, act_cols), lambda s, order, place: (0, 0)),
                pl.BlockSpec((1, piece, act_cols), lambda s, order, place: (order[s], 0, 0)),
                pl.BlockSpec((1, piece, act_cols), lambda s, order, place: (order[s], 0, 0)),
            ]
            + [pl.BlockSpec(part_block, lambda s, order, place: (x_of(place, s), 0, 0, 0))] * early
            + [pl.BlockSpec(acts_block, lambda s, order, place: (s, 0, 0, 0))] * 2,
            out_specs=[
                pl.BlockSpec(score_shape.shape, lambda s, order, place: (0, 0)),
                pl.BlockSpec(weighted_shape, lambda s, order, place: (0, 0, 0)),
            ],
            scratch_shapes=[
                pltpu.VMEM((early * 2 * blocks, targets * ROWS, act_cols), bf16),
                pltpu.VMEM((model_size * 2 * blocks,) + weighted_shape[1:], bf16),
                pltpu.VMEM(total_shape, jnp.float32),
            ],
        ),
        out_shape=[score_shape, jax.ShapeDtypeStruct(weighted_shape, bf16)],
        compiler_params=pltpu.CompilerParams(vmem_limit_bytes=60 * MIB),
        cost_estimate=pl.CostEstimate(flops=early * work, bytes_accessed=16 * MIB, transcendentals=0),
        name="first_scores",
    )(order, place, query_parts, chosen_acts, eigen_values[0], other_values,
      *grad_parts[:early], near, far)
    last_scores = pl.pallas_call(
        last_kernel,
        grid_spec=pltpu.PrefetchScalarGridSpec(
            num_scalar_prefetch=1,
            grid=(width,),
            in_specs=[
                pl.BlockSpec(part_block, lambda s, place: (x_of(place, s), 0, 0, 0)),
                pl.BlockSpec(acts_block, lambda s, place: (s, 0, 0, 0)),
                pl.BlockSpec(acts_block, lambda s, place: (s, 0, 0, 0)),
                pl.BlockSpec(memory_space=pl.ANY),
            ],
            out_specs=pl.BlockSpec(score_shape.shape, lambda s, place: (0, 0)),
            scratch_shapes=[
                pltpu.VMEM((2 * blocks, targets * ROWS, act_cols), bf16),
                pltpu.VMEM(weighted_shape, bf16),
                pltpu.VMEM(total_shape, jnp.float32),
                pltpu.SemaphoreType.DMA,
            ],
        ),
        out_shape=score_shape,
        compiler_params=pltpu.CompilerParams(vmem_limit_bytes=60 * MIB),
        cost_estimate=pl.CostEstimate(flops=work, bytes_accessed=9 * MIB, transcendentals=0),
        name="last_scores",
    )(place, opposite, near, far, last_weighted)
    scores = early_scores + last_scores
    partial = scores.reshape(targets, queries, ROWS).sum(axis=2)

    rows = partial.reshape(width, DEPTH // 2, 1, CORES, queries)
    parities = jnp.arange(2).reshape(1, 1, 2, 1, 1)
    rows = jnp.where(parities == my_class, rows, 0.0).reshape(data_size, 1, queries)
    rows = jnp.broadcast_to(rows, (data_size, model_size, queries))
    rows = rows.reshape(data_size * model_size, queries)
    rows = lax.all_to_all(rows, ("dp", "mp"), split_axis=0, concat_axis=0, tiled=True)
    mine = rows.sum(axis=0, keepdims=True)
    sections = lax.axis_size("section")
    swapped = [(i, (i + 1) % sections) for i in range(sections)]
    mine = mine + lax.ppermute(mine, "section", swapped)
    layers = train_acts.shape[0] * lax.axis_size("section")
    normalizer = math.sqrt(
        layers * act_cols * model_size * grad_cols * model_size * SEQLEN * length
    )
    return mine / normalizer


def solution(mesh):
    in_specs = (
        P("section", "dp", "mp"),
        P("section", "dp", "mp"),
        P("section", "mp", None),
        P("section", "mp", None),
        P("section", None, "dp", "mp"),
        P("section", "dp", None, "mp"),
        P("section", "dp", None, "mp"),
        P(),
    )
    return jax.shard_map(
        per_device, mesh=mesh, in_specs=in_specs, out_specs=P("dp", None), check_vma=False
    )
```
